128 devices in a mesh: dp: 2 (over z_lo), seq: 64 (over x, z_hi, y, core).
Axes of the slice: x: 4, y: 4, z: 4 (z_hi: 2, z_lo: 2; z = z_hi * 2 + z_lo), core: 2. Of those that a mesh axis runs over, the one named last changes fastest.
Arguments:
- query_raw: bfloat16 [2, 131072, 768], P('dp', 'seq'), may hold values from -6 to 6
- key_raw: bfloat16 [2, 131072, 768], P('dp', 'seq'), may hold values from -6 to 6
- value_raw: bfloat16 [2, 131072, 768], P('dp', 'seq'), may hold values from -6 to 6
- out_grad: bfloat16 [2, 131072, 768], P('dp', 'seq'), may hold values from -6 to 6
- conv_taps: float32 [3, 3, 768], replicated, may hold values from -3 to 3
- left_block: bfloat16 [512, 512], replicated, may hold values from -0.25 to 0.25
- right_block: bfloat16 [256, 256], replicated, may hold values from -0.375 to 0.375
- twiddle: float32 [256, 512], P('seq'), may hold values from 0.5 to 2
Outputs:
- query_grad: bfloat16 [2, 131072, 768], P('dp', 'seq')
- key_grad: bfloat16 [2, 131072, 768], P('dp', 'seq')
- value_grad: bfloat16 [2, 131072, 768], P('dp', 'seq')
- conv_grad: float32 [3, 3, 768], replicated
- left_grad: float32 [512, 512], replicated
- right_grad: float32 [256, 256], replicated
- twiddle_grad: float32 [256, 512], P('seq')
The draws below stay inside these ranges and needn't reach their ends.
All inputs are finite; a program needn't handle non-finite values.
Results may differ from the reference program's by a relative error of at most 0.0064.
Values may be sent and summed in bfloat16 or wider, within the bound.
A program may use at most 192 MiB of HBM per device.

```python
import jax
import jax.numpy as jnp

FACTOR_A = 256
FACTOR_B = 512
CHANNELS = 768
SEQ_LEN = 131072
BATCH_ALL = 2


def block_scale(stream_key, dims, shards, smallest, largest):
    level = 1.0
    for dim, shards_of in shards:
        steps = jax.random.uniform(jax.random.fold_in(jax.random.fold_in(stream_key, 6), dim), (shards_of,), jnp.float32, smallest / len(shards), largest / len(shards))
        level = level * jnp.repeat(jnp.exp(steps), dims[dim] // shards_of).reshape((-1,) + (1,) * (len(dims) - 1 - dim))
    return level


def gaussian(stream_key, extent, scale, reach, shards=(), dtype=jnp.bfloat16):
    factor_of = block_scale(stream_key, extent, shards, -0.22, 0.18) if shards else 1.0
    entries = jax.random.normal(stream_key, extent, jnp.float32) * scale * factor_of
    return jnp.minimum(jnp.maximum(entries, -reach), reach).astype(dtype)


def setup_inputs(seed: int = 0) -> dict:
    key_list = jax.random.split(jax.random.key(seed), 9)
    return {
        "query_raw": gaussian(key_list[0], (BATCH_ALL, SEQ_LEN, CHANNELS), 1.0, 6.0, ((0, 2), (1, 64))),
        "key_raw": gaussian(key_list[1], (BATCH_ALL, SEQ_LEN, CHANNELS), 1.0, 6.0, ((0, 2), (1, 64))),
        "value_raw": gaussian(key_list[2], (BATCH_ALL, SEQ_LEN, CHANNELS), 1.0, 6.0, ((0, 2), (1, 64))),
        "out_grad": gaussian(key_list[3], (BATCH_ALL, SEQ_LEN, CHANNELS), 1.0, 6.0, ((0, 2), (1, 64))),
        "conv_taps": gaussian(key_list[4], (3, 3, CHANNELS), 0.6, 3.0, (), jnp.float32),
        "left_block": gaussian(key_list[5], (FACTOR_B, FACTOR_B), FACTOR_B ** -0.5, 0.25),
        "right_block": gaussian(key_list[6], (FACTOR_A, FACTOR_A), FACTOR_A ** -0.5, 0.375),
        "twiddle": jnp.clip(0.5 + 1.5 * jax.random.uniform(key_list[7], (FACTOR_A, FACTOR_B), jnp.float32) ** block_scale(key_list[7], (FACTOR_A, FACTOR_B), ((0, 64),), -0.2, 0.2), 0.5, 2.0),
    }


def short_conv(values, tap_rows):
    padded = jnp.concatenate([jnp.zeros((2, values.shape[1]), jnp.float32), values], 0)
    return tap_rows[0] * padded[2:] + tap_rows[1] * padded[1:-1] + tap_rows[2] * padded[:-2]


def conv_back(grads, tap_rows):
    extended = jnp.concatenate([grads, jnp.zeros((2, grads.shape[1]), jnp.float32)], 0)
    return tap_rows[0] * extended[:-2] + tap_rows[1] * extended[1:-1] + tap_rows[2] * extended[2:]


def tap_terms(grads, values):
    padded = jnp.concatenate([jnp.zeros((2, values.shape[1]), jnp.float32), values], 0)
    return jnp.stack([jnp.sum(grads * padded[2:], 0), jnp.sum(grads * padded[1:-1], 0), jnp.sum(grads * padded[:-2], 0)])


def reference(query_raw, key_raw, value_raw, out_grad, conv_taps, left_block, right_block, twiddle):
    left_wide = left_block.astype(jnp.float32)
    right_wide = right_block.astype(jnp.float32)
    twist = twiddle[:, :, None]
    left_total = jnp.zeros((FACTOR_B, FACTOR_B), jnp.float32)
    right_total = jnp.zeros((FACTOR_A, FACTOR_A), jnp.float32)
    twist_total = jnp.zeros((FACTOR_A, FACTOR_B), jnp.float32)
    tap_total = jnp.zeros((3, 3, CHANNELS), jnp.float32)
    results = [[], [], []]
    for member in range(BATCH_ALL):
        raws = [query_raw[member].astype(jnp.float32), key_raw[member].astype(jnp.float32), value_raw[member].astype(jnp.float32)]
        q_conv = short_conv(raws[0], conv_taps[0])
        k_conv = short_conv(raws[1], conv_taps[1])
        v_conv = short_conv(raws[2], conv_taps[2])
        gated = (k_conv * v_conv).astype(jnp.bfloat16).reshape(FACTOR_A, FACTOR_B, CHANNELS).astype(jnp.float32)
        mixed = jnp.einsum('bd,adc->abc', left_wide, gated)
        scaled = (mixed * twist).astype(jnp.bfloat16).astype(jnp.float32)
        monarch = jnp.einsum('ae,ebc->abc', right_wide, scaled).astype(jnp.bfloat16).astype(jnp.float32)
        upstream = out_grad[member].astype(jnp.float32).reshape(FACTOR_A, FACTOR_B, CHANNELS)
        gate_grad = (upstream * q_conv.reshape(FACTOR_A, FACTOR_B, CHANNELS)).astype(jnp.bfloat16).astype(jnp.float32)
        q_conv_grad = (upstream * monarch).reshape(SEQ_LEN, CHANNELS)
        scaled_grad = jnp.einsum('ae,abc->ebc', right_wide, gate_grad).astype(jnp.bfloat16).astype(jnp.float32)
        right_total = right_total + jnp.einsum('abc,ebc->ae', gate_grad, scaled)
        twist_total = twist_total + jnp.sum(scaled_grad * mixed, axis=2)
        mixed_grad = (scaled_grad * twist).astype(jnp.bfloat16).astype(jnp.float32)
        gated_grad = jnp.einsum('bd,abc->adc', left_wide, mixed_grad).reshape(SEQ_LEN, CHANNELS)
        left_total = left_total + jnp.einsum('abc,adc->bd', mixed_grad, gated)
        grads = [q_conv_grad, gated_grad * v_conv, gated_grad * k_conv]
        for stream in range(3):
            results[stream].append(conv_back(grads[stream], conv_taps[stream]).astype(jnp.bfloat16))
            tap_total = tap_total.at[stream].add(tap_terms(grads[stream], raws[stream]))
    return (jnp.stack(results[0]), jnp.stack(results[1]), jnp.stack(results[2]), tap_total, left_total, right_total, twist_total)
```

```python
import jax
import jax.numpy as jnp
from jax import lax
from jax.experimental import pallas as pl
from jax.experimental.pallas import tpu as pltpu
from jax.sharding import PartitionSpec as P

F32, BF16 = jnp.float32, jnp.bfloat16
MESH = pl.DeviceIdType.MESH
SEQ, DP = 64, 2
DEVICES = SEQ * DP
ROWS, COLS, CH = 4, 512, 768
TOKENS = ROWS * COLS
CC = 256
NC = CH // CC
LANES = CC // 128
TILES = CH // 128
WHOLE = TOKENS + 16
VMEM_LIMIT = 62 * 2**20


def dot(a, b):
    return jnp.dot(a, b, preferred_element_type=F32)


def dot_nt(a, b):
    return lax.dot_general(a, b, (((1,), (1,)), ((), ())), preferred_element_type=F32)


def loop(lo, hi, body):
    def step(i, carry):
        body(i)
        return carry

    lax.fori_loop(lo, hi, step, 0)


def wide(column):
    return jnp.concatenate([column] * LANES, axis=1)


def kernel(
    q_in, k_in, v_in, o_in, taps, left, right, twist,
    q_out, k_out, v_out, conv_out, left_out, right_out, twist_out,
    xq, xk, xv, xo, gs, gr, br, ss, sr, mr, gd, gated, sd, zb, mg, gk, gv,
    obuf, mh, kh, perm, perm_t, left_t, right_t, twist_t, twist_acc, tws, twx,
    left_acc, right_acc, lx, lb, li, lsum, lg, lg2, rb, ri, rsum, rg,
    ckv, cq, ci, cj, csum, cg,
    in_sem, halo_s, halo_r, a2a_s, a2a_r, mh_s, mh_r, kh_s, kh_r, out_sem,
    l_s, l_r, r_s, r_r, c_s, c_r, tw_s, tw_r,
):
    d, s = lax.axis_index("dp"), lax.axis_index("seq")
    x, zh, y, core = s // 16, (s // 8) % 2, (s // 2) % 4, s % 2
    me = d * SEQ + s
    chip = d * 32 + s // 2
    first, last = s == 0, s == SEQ - 1

    def peer(i):
        o = (i * 9) % 64
        bit = [(o // (1 << n)) % 2 for n in range(6)]
        dx, dz, dy, dc = 2 * bit[0] + bit[2], bit[1], 2 * bit[3] + bit[4], bit[5]
        dx = dx + core * (4 - 2 * dx)
        dy = dy + core * (4 - 2 * dy)
        return (((x + dx) % 4 * 2 + (zh + dz) % 2) * 4 + (y + dy) % 4) * 2 + (core + dc) % 2

    def local(src, dst, sem):
        return pltpu.make_async_copy(src, dst, sem)

    def remote(src, dst, ssem, rsem, dev):
        return pltpu.make_async_remote_copy(
            src_ref=src, dst_ref=dst, send_sem=ssem, recv_sem=rsem, device_id=dev, device_id_type=MESH
        )

    def wait_bytes(ref, sem):
        pltpu.make_async_copy(ref, ref, sem).wait()

    def lane(cc):
        return pl.ds(cc * CC, CC)

    barrier = pltpu.get_barrier_semaphore()

    def greet(i):
        t = (me + i) % DEVICES
        pl.semaphore_signal(barrier, inc=1, device_id=(t // SEQ, t % SEQ), device_id_type=MESH)

    loop(1, DEVICES, greet)

    ins = (q_in, o_in, k_in, v_in)
    bufs = (xq, xo, xk, xv)

    def load(n, cc):
        row = 0 if n == 1 else 16
        return local(ins[n].at[:, lane(cc)], bufs[n].at[cc, pl.ds(row, TOKENS)], in_sem.at[n, cc])

    for pair in ((0, 1), (2, 3)):
        for cc in range(NC):
            for n in pair:
                load(n, cc).start()

    def halo(n, cc):
        if n == 1:
            return remote(o_in.at[pl.ds(0, 16), lane(cc)], xo.at[cc, pl.ds(TOKENS, 16)],
                          halo_s.at[n, cc], halo_r.at[n, cc], (d, jnp.maximum(s - 1, 0)))
        return remote(ins[n].at[pl.ds(TOKENS - 16, 16), lane(cc)], bufs[n].at[cc, pl.ds(0, 16)],
                      halo_s.at[n, cc], halo_r.at[n, cc], (d, jnp.minimum(s + 1, SEQ - 1)))

    @pl.when(first)
    def _():
        for ref in (xq, xk, xv):
            ref[:, 0:16, :] = jnp.zeros((NC, 16, CC), BF16)

    @pl.when(last)
    def _():
        xo[:, TOKENS:WHOLE, :] = jnp.zeros((NC, 16, CC), BF16)
        mh[...] = jnp.zeros_like(mh)
        kh[...] = jnp.zeros_like(kh)

    def tap(stream, j, cc):
        return taps[stream, j : j + 1, cc * CC : (cc + 1) * CC]

    def shifts(ref, cc, r, n):
        wide_x = ref[cc, pl.ds(r, n + 16), :].astype(F32)
        return wide_x[16:], wide_x[15:-1], wide_x[14:-2]

    def conv(ref, cc, r, n, stream):
        x0, x1, x2 = shifts(ref, cc, r, n)
        return tap(stream, 0, cc) * x0 + tap(stream, 1, cc) * x1 + tap(stream, 2, cc) * x2

    def gate_block(cc, blk):
        h, i = blk // 4, blk % 4
        parts = []
        for e in range(2):
            r = pl.multiple_of((2 * h + e) * COLS + i * 128, 128)
            g = xo[cc, pl.ds(r, 128), :].astype(F32) * conv(xq, cc, r, 128, 0)
            parts.append(g.reshape(16, 8, CC))
        gs[cc, pl.ds(i * 16, 16), pl.ds(pl.multiple_of(h * 16, 16), 16), :] = jnp.concatenate(parts, 1).astype(BF16)

    def exchange(phase, src, dst, cc):
        def send(i):
            t = peer(i)
            remote(src.at[cc, t], dst.at[cc, s], a2a_s.at[phase, cc], a2a_r.at[phase, cc], (d, t)).start()

        loop(1, SEQ, send)
        local(src.at[cc, s], dst.at[cc, s], a2a_r.at[phase, cc]).start()

    def arrived(phase, dst, cc):
        wait_bytes(dst.at[cc], a2a_r.at[phase, cc])

    def halo_wait(n, cc):
        @pl.when(jnp.logical_not(last if n == 1 else first))
        def _():
            halo(n, cc).wait_recv()

    load(0, 0).wait()
    load(1, 0).wait()
    loop(0, 7, lambda n: gate_block(0, 7 - n))
    pl.semaphore_wait(barrier, DEVICES - 1)
    for n in (0, 2, 3):
        @pl.when(jnp.logical_not(last))
        def _():
            for cc in range(NC):
                halo(n, cc).start()

    @pl.when(jnp.logical_not(first))
    def _():
        for cc in range(NC):
            halo(1, cc).start()

    halo_wait(0, 0)
    gate_block(0, 0)
    exchange(0, gs, gr, 0)
    for cc in range(1, NC):
        load(0, cc).wait()
        load(1, cc).wait()
        halo_wait(0, cc)
        loop(0, 8, lambda n: gate_block(cc, n))
        exchange(0, gs, gr, cc)

    row = lax.broadcasted_iota(jnp.int32, (256, 256), 0)
    col = lax.broadcasted_iota(jnp.int32, (256, 256), 1)
    perm[...] = jnp.where(col == (row & 31) * 8 + (row >> 5), 1.0, 0.0).astype(BF16)
    perm_t[...] = jnp.where(row == (col & 31) * 8 + (col >> 5), 1.0, 0.0).astype(BF16)
    left_t[...] = jnp.transpose(left[...].astype(F32)).astype(BF16)
    right_t[...] = jnp.transpose(right[...].astype(F32)).astype(BF16)
    for a in range(ROWS):
        twist_t[a] = jnp.transpose(jnp.broadcast_to(twist[a : a + 1, :], (128, COLS)))
    twist_acc[...] = jnp.zeros_like(twist_acc)
    left_acc[...] = jnp.zeros_like(left_acc)
    right_acc[...] = jnp.zeros_like(right_acc)
    ckv[...] = jnp.zeros_like(ckv)
    cq[...] = jnp.zeros_like(cq)
    tws[...] = jnp.zeros_like(tws)

    def scaled(cc):
        def make_gated(blk):
            a, i = blk // 4, blk % 4
            r = pl.multiple_of(blk * 128, 128)
            gated[cc, a, pl.ds(pl.multiple_of(i * 128, 128), 128), :] = (
                conv(xk, cc, r, 128, 1) * conv(xv, cc, r, 128, 2)
            ).astype(BF16)

        loop(0, 16, make_gated)

        def mix(blk):
            h, i = blk // 2, blk % 2
            b = pl.ds(pl.multiple_of(i * 256, 256), 256)
            parts = []
            for e in range(2):
                m = dot(left[b, :], gated[cc, 2 * h + e]) * wide(twist_t[2 * h + e, b, :])
                parts.append(m.reshape(32, 8, CC))
            ss[cc, pl.ds(i * 32, 32), pl.ds(pl.multiple_of(h * 16, 16), 16), :] = jnp.concatenate(parts, 1).astype(BF16)

        loop(0, 4, mix)

    for cc in range(NC):
        for n in (2, 3):
            load(n, cc).wait()
            halo_wait(n, cc)
        scaled(cc)

    def spread(src, cc, put):
        def go(g):
            block = src[cc, pl.ds(g * 8, 8), :, :].reshape(256, CC)
            put(g, dot(perm[...], block).astype(BF16).reshape(8, 32, CC))

        loop(0, 8, go)

    def gather_back(dst, cc):
        def go(g):
            block = zb[:, pl.ds(pl.multiple_of(g * 32, 32), 32), :].reshape(256, CC)
            dst[cc, pl.ds(g * 8, 8), :, :] = dot(perm_t[...], block).astype(BF16).reshape(8, 32, CC)

        loop(0, 8, go)

    for cc in range(NC):
        arrived(0, gr, cc)

        def put_gd(g, value):
            gd[cc, :, pl.ds(pl.multiple_of(g * 32, 32), 32), :] = value

        spread(gr, cc, put_gd)

        def back_mul(b):
            zb[b] = dot(right_t[...], gd[cc, b]).astype(BF16)

        loop(0, 8, back_mul)
        gather_back(gr, cc)
        exchange(1, gr, br, cc)
    for cc in range(NC):
        exchange(2, ss, sr, cc)

    def after_rows(cc, stream, which):
        return remote(which.at[cc % 2, pl.ds(0, 8)], kh.at[cc, stream], kh_s.at[cc, stream], kh_r.at[cc, stream],
                      (d, jnp.maximum(s - 1, 0)))

    def kv_first(cc):
        par = cc % 2
        arrived(1, br, cc)

        def unpack(blk):
            h, i = blk // 4, blk % 4
            peers, half = pl.ds(i * 16, 16), pl.ds(pl.multiple_of(h * 16, 16), 16)
            b = pl.ds(pl.multiple_of(i * 128, 128), 128)
            grads, products = br[cc, peers, half, :].astype(F32), ss[cc, peers, half, :].astype(F32)
            for e in range(2):
                a = 2 * h + e
                g = grads[:, 8 * e : 8 * e + 8].reshape(128, CC)
                p = g * products[:, 8 * e : 8 * e + 8].reshape(128, CC)
                total = p[:, :128]
                for n in range(1, LANES):
                    total = total + p[:, n * 128 : (n + 1) * 128]
                twist_acc[a, b, :] += total
                mg[a, b, :] = (g * wide(twist_t[a, b, :])).astype(BF16)

        loop(0, 8, unpack)

        def left_terms(blk):
            a, i = blk // 2, blk % 2
            b = pl.ds(pl.multiple_of(i * 256, 256), 256)
            left_acc[b, :] += dot_nt(mg[a, b, :], gated[cc, a])

        loop(0, 8, left_terms)

        def back(blk):
            a, i = blk // 2, blk % 2
            r = pl.multiple_of(blk * 256, 256)
            g = dot(left_t[pl.ds(pl.multiple_of(i * 256, 256), 256), :], mg[a])
            gk[par, pl.ds(r, 256), :] = g * conv(xv, cc, r, 256, 2)
            gv[par, pl.ds(r, 256), :] = g * conv(xk, cc, r, 256, 1)

        loop(0, 8, back)

        @pl.when(jnp.logical_not(first))
        def _():
            after_rows(cc, 0, gk).start()
            after_rows(cc, 1, gv).start()

    def conv_back(grad, par, ref, cc, stream, total_ref, base):
        def step(blk, sums):
            r = pl.multiple_of(blk * 128, 128)
            g = grad[par, pl.ds(r, 136), :]
            obuf[stream, pl.ds(r, 128), :] = (
                tap(stream, 0, cc) * g[:128] + tap(stream, 1, cc) * g[1:129] + tap(stream, 2, cc) * g[2:130]
            ).astype(BF16)
            shifted = shifts(ref, cc, r, 128)
            return tuple(
                sums[j] + jnp.sum((g[:128] * shifted[j]).reshape(16, 8, CC), axis=0) for j in range(3)
            )

        sums = lax.fori_loop(0, 16, step, tuple(jnp.zeros((8, CC), F32) for _ in range(3)))
        for j in range(3):
            total = jnp.sum(sums[j], axis=0, keepdims=True)
            for n in range(LANES):
                total_ref[cc * LANES + n, base + j : base + j + 1, :] = total[:, n * 128 : (n + 1) * 128]

    outs = (q_out, k_out, v_out)

    def store(stream, cc):
        return local(obuf.at[stream], outs[stream].at[:, lane(cc)], out_sem.at[stream, cc])

    def finish(grad, par, ref, cc, stream, total_ref, base):
        if cc:
            store(stream, cc - 1).wait()
        conv_back(grad, par, ref, cc, stream, total_ref, base)
        store(stream, cc).start()

    def kv_second(cc):
        par = cc % 2

        @pl.when(jnp.logical_not(last))
        def _():
            after_rows(cc, 0, gk).wait_recv()
            after_rows(cc, 1, gv).wait_recv()

        @pl.when(jnp.logical_not(first))
        def _():
            after_rows(cc, 0, gk).wait_send()
            after_rows(cc, 1, gv).wait_send()

        gk[par, TOKENS : TOKENS + 8, :] = kh[cc, 0]
        gv[par, TOKENS : TOKENS + 8, :] = kh[cc, 1]
        finish(gk, par, xk, cc, 1, ckv, 0)
        finish(gv, par, xv, cc, 2, ckv, 3)

    def monarch(cc):
        arrived(2, sr, cc)

        def put_sd(g, value):
            sd[:, pl.ds(pl.multiple_of(g * 32, 32), 32), :] = value

        spread(sr, cc, put_sd)

        def mul(b):
            zb[b] = dot(right[...], sd[b]).astype(BF16)
            right_acc[...] += dot_nt(gd[cc, b], sd[b])

        loop(0, 8, mul)
        gather_back(sr, cc)

    def send_monarch(cc):
        exchange(3, sr, mr, cc)

        @pl.when(first)
        def _():
            def also(t):
                remote(sr.at[cc, t + 1, pl.ds(0, 16)], mh.at[cc], mh_s.at[cc], mh_r.at[cc], (d, t)).start()

            loop(1, SEQ - 1, also)
            local(sr.at[cc, 1, pl.ds(0, 16)], mh.at[cc], mh_r.at[cc]).start()

    partner = s + 1 - 2 * core

    def pair_copy():
        return remote(left_acc.at[pl.ds(pl.multiple_of((1 - core) * 256, 256), 256)], lx, l_s.at[0], l_r.at[0], (d, partner))

    def chip_of(i):
        t = (chip + i * 23) % 64
        return t, (t // 32, (t % 32) * 2 + core)

    def left_scatter():
        pair_copy().wait()
        half = left_acc[pl.ds(pl.multiple_of(core * 256, 256), 256), :] + lx[...]
        for n in range(4):
            lb[:, n] = half[:, n * 128 : (n + 1) * 128].astype(BF16).reshape(16, 16, 128)

        def send(i):
            t, dev = chip_of(i)
            remote(lb.at[t // 4, t % 4], li.at[chip], l_s.at[1], l_r.at[1], dev).start()

        loop(1, 64, send)
        local(lb.at[chip // 4, chip % 4], li.at[chip], l_r.at[1]).start()

    def left_gather():
        wait_bytes(li, l_r.at[1])
        lsum[...] = jnp.sum(li[...].astype(F32), axis=0).astype(BF16)

        def send(i):
            t, dev = chip_of(i)
            remote(lsum, lg.at[chip], l_s.at[2], l_r.at[2], dev).start()

        loop(1, 64, send)
        local(lsum, lg.at[chip], l_r.at[2]).start()

    def left_pair():
        return remote(lg, lg2, l_s.at[3], l_r.at[3], (d, partner))

    def left_finish():
        left_pair().wait()
        mine = lg[...].reshape(16, 4, 16, 128)
        other = lg2[...].reshape(16, 4, 16, 128)
        for n in range(4):
            left_out[pl.ds(pl.multiple_of(core * 256, 256), 256), n * 128 : (n + 1) * 128] = (
                mine[:, n].reshape(256, 128).astype(F32)
            )
            left_out[pl.ds(pl.multiple_of((1 - core) * 256, 256), 256), n * 128 : (n + 1) * 128] = (
                other[:, n].reshape(256, 128).astype(F32)
            )

    def to_owners(count, owner, src, inbox, ssem, rsem):
        def send(n):
            t = (n + me) % count
            dev = owner(t)

            @pl.when(dev == me)
            def _():
                local(src(t), inbox.at[me], rsem).start()

            @pl.when(dev != me)
            def _():
                remote(src(t), inbox.at[me], ssem, rsem, (dev // SEQ, dev % SEQ)).start()

        loop(0, count, send)

    def from_owner(count, owner, inbox, total, spread_to, rsem_in, ssem, rsem):
        def each(t):
            @pl.when(owner(t) == me)
            def _():
                wait_bytes(inbox, rsem_in)
                total[...] = jnp.sum(inbox[...].astype(F32), axis=0).astype(total.dtype)

                def send(i):
                    dev = (me + i * 37) % DEVICES
                    remote(total, spread_to.at[t], ssem, rsem, (dev // SEQ, dev % SEQ)).start()

                loop(1, DEVICES, send)
                local(total, spread_to.at[t], rsem).start()

        loop(0, count, each)

    def sent_to_owners(count, owner, src, ssem):
        def each(t):
            @pl.when(owner(t) != me)
            def _():
                wait_bytes(src.at[0], ssem)

        loop(0, count, each)

    def sent_by_owner(count, owner, inbox, ssem):
        def each(t):
            @pl.when(owner(t) == me)
            def _():
                wait_bytes(inbox.at[pl.ds(0, DEVICES - 1)], ssem)

        loop(0, count, each)

    def right_owner(t):
        n = t // 2
        return (t % 2) * SEQ + n * 4 + n % 4

    def kv_owner(t):
        return (t % 2) * SEQ + t * 10 + 3

    def q_owner(t):
        return ((t + 1) % 2) * SEQ + t * 10 + 8

    kv_first(0)
    kv_first(1)
    kv_second(0)
    kv_first(2)
    pair_copy().start()
    for a in range(ROWS):
        tws[a : a + 1, :] = jnp.sum(jnp.transpose(twist_acc[a]), axis=0, keepdims=True)
    twist_copy = remote(tws, twx, tw_s, tw_r, (1 - d, s))
    twist_copy.start()
    left_scatter()
    monarch(0)
    send_monarch(0)
    kv_second(1)
    monarch(1)
    send_monarch(1)
    kv_second(2)
    to_owners(TILES, kv_owner, lambda t: ckv.at[t], ci, c_s.at[0], c_r.at[0])
    left_gather()
    monarch(2)
    for n in range(2):
        rb[:, n] = right_acc[:, n * 128 : (n + 1) * 128].astype(BF16).reshape(16, 16, 128)
    to_owners(32, right_owner, lambda t: rb.at[t // 2, t % 2], ri, r_s.at[0], r_r.at[0])
    send_monarch(2)

    def query(cc):
        par = cc % 2
        arrived(3, mr, cc)

        @pl.when(jnp.logical_not(last))
        def _():
            wait_bytes(mh.at[cc], mh_r.at[cc])

        def unpack(blk):
            h, i = blk // 4, blk % 4
            m = mr[cc, pl.ds(i * 16, 16), pl.ds(pl.multiple_of(h * 16, 16), 16), :].astype(F32)
            for e in range(2):
                r = pl.multiple_of((2 * h + e) * COLS + i * 128, 128)
                gk[par, pl.ds(r, 128), :] = xo[cc, pl.ds(r, 128), :].astype(F32) * m[:, 8 * e : 8 * e + 8].reshape(128, CC)

        loop(0, 8, unpack)
        tail = xo[cc, TOKENS:WHOLE, :].astype(F32) * mh[cc].astype(F32)
        gk[par, TOKENS : TOKENS + 8, :] = tail[:8]
        finish(gk, par, xq, cc, 0, cq, 0)

    halo_wait(1, 0)
    query(0)
    from_owner(TILES, kv_owner, ci, csum.at[0], cg.at[0], c_r.at[0], c_s.at[1], c_r.at[1])
    halo_wait(1, 1)
    query(1)
    from_owner(32, right_owner, ri, rsum, rg, r_r.at[0], r_s.at[1], r_r.at[1])
    wait_bytes(lg, l_r.at[2])
    left_pair().start()
    twist_copy.wait()
    twist_out[...] = (tws[0:ROWS, :] + twx[0:ROWS, :]) / twist[...]
    halo_wait(1, 2)
    query(2)
    to_owners(TILES, q_owner, lambda t: cq.at[t], cj, c_s.at[2], c_r.at[2])
    left_finish()
    from_owner(TILES, q_owner, cj, csum.at[1], cg.at[1], c_r.at[2], c_s.at[3], c_r.at[3])
    wait_bytes(rg, r_r.at[1])
    for n in range(2):
        right_out[:, n * 128 : (n + 1) * 128] = (
            rg[...].reshape(16, 2, 16, 128)[:, n].reshape(256, 128).astype(F32)
        )
    wait_bytes(cg.at[0], c_r.at[1])
    wait_bytes(cg.at[1], c_r.at[3])
    for t in range(TILES):
        lanes = slice(t * 128, (t + 1) * 128)
        conv_out[0, :, lanes] = cg[1, t, 0:3, :]
        conv_out[1, :, lanes] = cg[0, t, 0:3, :]
        conv_out[2, :, lanes] = cg[0, t, 3:6, :]

    for stream in range(3):
        store(stream, NC - 1).wait()
    for phase, src in enumerate((gs, gr, ss, sr)):
        for cc in range(NC):
            wait_bytes(src.at[cc, pl.ds(0, SEQ - 1)], a2a_s.at[phase, cc])

    @pl.when(jnp.logical_not(last))
    def _():
        for n in (0, 2, 3):
            for cc in range(NC):
                halo(n, cc).wait_send()

    @pl.when(jnp.logical_not(first))
    def _():
        for cc in range(NC):
            halo(1, cc).wait_send()

    @pl.when(first)
    def _():
        for cc in range(NC):
            wait_bytes(sr.at[cc, pl.ds(0, SEQ - 2), pl.ds(0, 16)], mh_s.at[cc])

    wait_bytes(li.at[pl.ds(0, 63)], l_s.at[1])
    wait_bytes(li.at[pl.ds(0, 63)], l_s.at[2])
    sent_to_owners(32, right_owner, ri, r_s.at[0])
    sent_by_owner(32, right_owner, ri, r_s.at[1])
    sent_to_owners(TILES, kv_owner, ci, c_s.at[0])
    sent_by_owner(TILES, kv_owner, ci, c_s.at[1])
    sent_to_owners(TILES, q_owner, cj, c_s.at[2])
    sent_by_owner(TILES, q_owner, cj, c_s.at[3])


def vmem(*shape, dtype=BF16):
    return pltpu.VMEM(shape, dtype)


def dma(*shape):
    return pltpu.SemaphoreType.DMA(shape)


def shards(query_raw, key_raw, value_raw, out_grad, conv_taps, left_block, right_block, twiddle):
    flat = [a.reshape(TOKENS, CH) for a in (query_raw, key_raw, value_raw, out_grad)]
    anywhere, inside = pl.BlockSpec(memory_space=pl.ANY), pl.BlockSpec(memory_space=pltpu.VMEM)
    staged = vmem(NC, SEQ, 32, CC)
    scratch = (
        [vmem(NC, WHOLE, CC)] * 4
        + [staged] * 6
        + [vmem(NC, 8, 256, CC), vmem(NC, ROWS, COLS, CC), vmem(8, 256, CC), vmem(8, 256, CC), vmem(ROWS, COLS, CC)]
        + [vmem(2, TOKENS + 8, CC, dtype=F32)] * 2
        + [vmem(3, TOKENS, CC), vmem(NC, 16, CC), vmem(NC, 2, 8, CC, dtype=F32)]
        + [vmem(256, 256), vmem(256, 256), vmem(COLS, COLS), vmem(256, 256)]
        + [vmem(ROWS, COLS, 128, dtype=F32)] * 2
        + [vmem(8, COLS, dtype=F32)] * 2
        + [vmem(COLS, COLS, dtype=F32), vmem(256, 256, dtype=F32), vmem(256, COLS, dtype=F32)]
        + [vmem(16, 4, 16, 128), vmem(64, 16, 128), vmem(16, 128), vmem(64, 16, 128), vmem(64, 16, 128)]
        + [vmem(16, 2, 16, 128), vmem(DEVICES, 16, 128), vmem(16, 128), vmem(32, 16, 128)]
        + [vmem(TILES, 8, 128, dtype=F32)] * 2
        + [vmem(DEVICES, 8, 128, dtype=F32)] * 2
        + [vmem(2, 8, 128, dtype=F32), vmem(2, TILES, 8, 128, dtype=F32)]
        + [dma(4, NC), dma(4, NC), dma(4, NC), dma(4, NC), dma(4, NC), dma(NC), dma(NC), dma(NC, 2), dma(NC, 2), dma(3, NC)]
        + [dma(4), dma(4), dma(2), dma(2), dma(4), dma(4), dma(), dma()]
    )
    results = pl.pallas_call(
        kernel,
        name="monarch_back",
        out_shape=[
            jax.ShapeDtypeStruct((TOKENS, CH), BF16),
            jax.ShapeDtypeStruct((TOKENS, CH), BF16),
            jax.ShapeDtypeStruct((TOKENS, CH), BF16),
            jax.ShapeDtypeStruct((3, 3, CH), F32),
            jax.ShapeDtypeStruct((COLS, COLS), F32),
            jax.ShapeDtypeStruct((256, 256), F32),
            jax.ShapeDtypeStruct((ROWS, COLS), F32),
        ],
        in_specs=[anywhere] * 4 + [inside] * 4,
        out_specs=[anywhere] * 3 + [inside] * 4,
        scratch_shapes=scratch,
        compiler_params=pltpu.CompilerParams(
            collective_id=0, has_side_effects=True, vmem_limit_bytes=VMEM_LIMIT
        ),
    )(flat[0], flat[1], flat[2], flat[3], conv_taps, left_block, right_block, twiddle)
    return tuple(r.reshape(1, TOKENS, CH) for r in results[:3]) + tuple(results[3:])


def solution(mesh):
    rows = P("dp", "seq", None)
    return jax.shard_map(
        shards,
        mesh=mesh,
        in_specs=(rows, rows, rows, rows, P(), P(), P(), P("seq", None)),
        out_specs=(rows, rows, rows, P(), P(), P(), P("seq", None)),
        check_vma=False,
    )
```

```python
import jax
import jax.numpy as jnp
from jax import lax
from jax.experimental import pallas as pl
from jax.experimental.pallas import tpu as pltpu
from jax.sharding import PartitionSpec as P

F32, BF16 = jnp.float32, jnp.bfloat16
MESH = pl.DeviceIdType.MESH
SEQ, DP = 64, 2
DEVICES = SEQ * DP
ROWS, COLS, CH = 4, 512, 768
TOKENS = ROWS * COLS
CC = 256
NC = CH // CC
LANES = CC // 128
TILES = CH // 128
WHOLE = TOKENS + 16
VMEM_LIMIT = 62 * 2**20


def dot(a, b):
    return jnp.dot(a, b, preferred_element_type=F32)


def dot_nt(a, b):
    return lax.dot_general(a, b, (((1,), (1,)), ((), ())), preferred_element_type=F32)


def loop(lo, hi, body):
    def step(i, carry):
        body(i)
        return carry

    lax.fori_loop(lo, hi, step, 0)


def wide(column):
    return jnp.concatenate([column] * LANES, axis=1)


def kernel(
    q_in, k_in, v_in, o_in, taps, left, right, twist,
    q_out, k_out, v_out, conv_out, left_out, right_out, twist_out,
    xq, xk, xv, xo, gs, gr, br, ss, sr, mr, gd, gated, sd, zb, mg, gk, gv,
    obuf, mh, kh, perm, perm_t, left_t, right_t, twist_t, twist_acc, tws, twx,
    left_acc, right_acc, lx, lb, li, lsum, lg, lg2, rx, kx, rb, ri, rsum, rg, rg2,
    ckv, cq, cq_last, ia, ia_last, ib, ib_last, sb, sb_last,
    in_sem, halo_s, halo_r, a2a_s, a2a_r, mh_s, mh_r, kh_s, kh_r, out_sem,
    l_s, l_r, r_s, r_r, c_s, c_r, tw_s, tw_r, q_s, q_r,
):
    d, s = lax.axis_index("dp"), lax.axis_index("seq")
    x, zh, y, core = s // 16, (s // 8) % 2, (s // 2) % 4, s % 2
    me = d * SEQ + s
    chip = d * 32 + s // 2
    first, last = s == 0, s == SEQ - 1

    def peer(i):
        o = (i * 9) % 64
        bit = [(o // (1 << n)) % 2 for n in range(6)]
        dx, dz, dy, dc = 2 * bit[0] + bit[2], bit[1], 2 * bit[3] + bit[4], bit[5]
        dx = dx + core * (4 - 2 * dx)
        dy = dy + core * (4 - 2 * dy)
        return (((x + dx) % 4 * 2 + (zh + dz) % 2) * 4 + (y + dy) % 4) * 2 + (core + dc) % 2

    def local(src, dst, sem):
        return pltpu.make_async_copy(src, dst, sem)

    def remote(src, dst, ssem, rsem, dev):
        return pltpu.make_async_remote_copy(
            src_ref=src, dst_ref=dst, send_sem=ssem, recv_sem=rsem, device_id=dev, device_id_type=MESH
        )

    def wait_bytes(ref, sem):
        pltpu.make_async_copy(ref, ref, sem).wait()

    def lane(cc):
        return pl.ds(cc * CC, CC)

    barrier = pltpu.get_barrier_semaphore()

    def greet(i):
        t = (me + i) % DEVICES
        pl.semaphore_signal(barrier, inc=1, device_id=(t // SEQ, t % SEQ), device_id_type=MESH)

    loop(1, DEVICES, greet)

    ins = (q_in, o_in, k_in, v_in)
    bufs = (xq, xo, xk, xv)

    def load(n, cc):
        row = 0 if n == 1 else 16
        return local(ins[n].at[:, lane(cc)], bufs[n].at[cc, pl.ds(row, TOKENS)], in_sem.at[n, cc])

    for pair in ((0, 1), (2, 3)):
        for cc in range(NC):
            for n in pair:
                load(n, cc).start()

    def halo(n, cc):
        if n == 1:
            return remote(o_in.at[pl.ds(0, 16), lane(cc)], xo.at[cc, pl.ds(TOKENS, 16)],
                          halo_s.at[n, cc], halo_r.at[n, cc], (d, jnp.maximum(s - 1, 0)))
        return remote(ins[n].at[pl.ds(TOKENS - 16, 16), lane(cc)], bufs[n].at[cc, pl.ds(0, 16)],
                      halo_s.at[n, cc], halo_r.at[n, cc], (d, jnp.minimum(s + 1, SEQ - 1)))

    @pl.when(first)
    def _():
        for ref in (xq, xk, xv):
            ref[:, 0:16, :] = jnp.zeros((NC, 16, CC), BF16)

    @pl.when(last)
    def _():
        xo[:, TOKENS:WHOLE, :] = jnp.zeros((NC, 16, CC), BF16)
        mh[...] = jnp.zeros_like(mh)
        kh[...] = jnp.zeros_like(kh)

    def tap(stream, j, cc, lo=0, hi=CC):
        return taps[stream, j : j + 1, cc * CC + lo : cc * CC + hi]

    def shifts(ref, cc, r, n, lo=0, hi=CC):
        wide_x = ref[cc, pl.ds(r, n + 16), lo:hi].astype(F32)
        return wide_x[16:], wide_x[15:-1], wide_x[14:-2]

    def conv(ref, cc, r, n, stream):
        x0, x1, x2 = shifts(ref, cc, r, n)
        return tap(stream, 0, cc) * x0 + tap(stream, 1, cc) * x1 + tap(stream, 2, cc) * x2

    def gate_block(cc, blk):
        h, i = blk // 4, blk % 4
        parts = []
        for e in range(2):
            r = pl.multiple_of((2 * h + e) * COLS + i * 128, 128)
            g = xo[cc, pl.ds(r, 128), :].astype(F32) * conv(xq, cc, r, 128, 0)
            parts.append(g.reshape(16, 8, CC))
        gs[cc, pl.ds(i * 16, 16), pl.ds(pl.multiple_of(h * 16, 16), 16), :] = jnp.concatenate(parts, 1).astype(BF16)

    def exchange(phase, src, dst, cc, lanes=slice(None)):
        def part(ref, t):
            return ref.at[cc, t, :, lanes]

        def send(i):
            t = peer(i)
            remote(part(src, t), part(dst, s), a2a_s.at[phase, cc], a2a_r.at[phase, cc], (d, t)).start()

        loop(1, SEQ, send)
        local(part(src, s), part(dst, s), a2a_r.at[phase, cc]).start()

    def arrived(phase, dst, cc, lanes=slice(None)):
        wait_bytes(dst.at[cc, :, :, lanes], a2a_r.at[phase, cc])

    def halo_wait(n, cc):
        @pl.when(jnp.logical_not(last if n == 1 else first))
        def _():
            halo(n, cc).wait_recv()

    load(0, 0).wait()
    load(1, 0).wait()
    loop(0, 7, lambda n: gate_block(0, 7 - n))
    pl.semaphore_wait(barrier, DEVICES - 1)
    for n in (0, 2, 3):
        @pl.when(jnp.logical_not(last))
        def _():
            for cc in range(NC):
                halo(n, cc).start()

    @pl.when(jnp.logical_not(first))
    def _():
        for cc in range(NC):
            halo(1, cc).start()

    halo_wait(0, 0)
    gate_block(0, 0)
    exchange(0, gs, gr, 0)
    for cc in range(1, NC):
        load(0, cc).wait()
        load(1, cc).wait()
        halo_wait(0, cc)
        loop(0, 8, lambda n: gate_block(cc, n))
        exchange(0, gs, gr, cc)

    row = lax.broadcasted_iota(jnp.int32, (256, 256), 0)
    col = lax.broadcasted_iota(jnp.int32, (256, 256), 1)
    perm[...] = jnp.where(col == (row & 31) * 8 + (row >> 5), 1.0, 0.0).astype(BF16)
    perm_t[...] = jnp.where(row == (col & 31) * 8 + (col >> 5), 1.0, 0.0).astype(BF16)
    left_t[...] = jnp.transpose(left[...].astype(F32)).astype(BF16)
    right_t[...] = jnp.transpose(right[...].astype(F32)).astype(BF16)
    for a in range(ROWS):
        twist_t[a] = jnp.transpose(jnp.broadcast_to(twist[a : a + 1, :], (128, COLS)))
    twist_acc[...] = jnp.zeros_like(twist_acc)
    left_acc[...] = jnp.zeros_like(left_acc)
    right_acc[...] = jnp.zeros_like(right_acc)
    ckv[...] = jnp.zeros_like(ckv)
    cq[...] = jnp.zeros_like(cq)
    cq_last[...] = jnp.zeros_like(cq_last)
    tws[...] = jnp.zeros_like(tws)
    rb[...] = jnp.zeros_like(rb)

    def scaled(cc):
        def make_gated(blk):
            a, i = blk // 4, blk % 4
            r = pl.multiple_of(blk * 128, 128)
            gated[cc, a, pl.ds(pl.multiple_of(i * 128, 128), 128), :] = (
                conv(xk, cc, r, 128, 1) * conv(xv, cc, r, 128, 2)
            ).astype(BF16)

        loop(0, 16, make_gated)

        def mix(blk):
            h, i = blk // 2, blk % 2
            b = pl.ds(pl.multiple_of(i * 256, 256), 256)
            parts = []
            for e in range(2):
                m = dot(left[b, :], gated[cc, 2 * h + e]) * wide(twist_t[2 * h + e, b, :])
                parts.append(m.reshape(32, 8, CC))
            ss[cc, pl.ds(i * 32, 32), pl.ds(pl.multiple_of(h * 16, 16), 16), :] = jnp.concatenate(parts, 1).astype(BF16)

        loop(0, 4, mix)

    for cc in range(NC):
        for n in (2, 3):
            load(n, cc).wait()
            halo_wait(n, cc)
        scaled(cc)

    def spread(src, cc, put):
        def go(g):
            block = src[cc, pl.ds(g * 8, 8), :, :].reshape(256, CC)
            put(g, dot(perm[...], block).astype(BF16).reshape(8, 32, CC))

        loop(0, 8, go)

    def gather_back(dst, cc):
        def go(g):
            block = zb[:, pl.ds(pl.multiple_of(g * 32, 32), 32), :].reshape(256, CC)
            dst[cc, pl.ds(g * 8, 8), :, :] = dot(perm_t[...], block).astype(BF16).reshape(8, 32, CC)

        loop(0, 8, go)

    for cc in range(NC):
        arrived(0, gr, cc)

        def put_gd(g, value):
            gd[cc, :, pl.ds(pl.multiple_of(g * 32, 32), 32), :] = value

        spread(gr, cc, put_gd)

        def back_mul(b):
            zb[b] = dot(right_t[...], gd[cc, b]).astype(BF16)

        loop(0, 8, back_mul)
        gather_back(gr, cc)
        exchange(1, gr, br, cc)
    for cc in range(NC):
        exchange(2, ss, sr, cc)

    def after_rows(cc, stream, which):
        return remote(which.at[cc % 2, pl.ds(0, 8)], kh.at[cc, stream], kh_s.at[cc, stream], kh_r.at[cc, stream],
                      (d, jnp.maximum(s - 1, 0)))

    def kv_first(cc):
        par = cc % 2
        arrived(1, br, cc)

        def unpack(blk):
            h, i = blk // 4, blk % 4
            peers, half = pl.ds(i * 16, 16), pl.ds(pl.multiple_of(h * 16, 16), 16)
            b = pl.ds(pl.multiple_of(i * 128, 128), 128)
            grads, products = br[cc, peers, half, :].astype(F32), ss[cc, peers, half, :].astype(F32)
            for e in range(2):
                a = 2 * h + e
                g = grads[:, 8 * e : 8 * e + 8].reshape(128, CC)
                p = g * products[:, 8 * e : 8 * e + 8].reshape(128, CC)
                total = p[:, :128]
                for n in range(1, LANES):
                    total = total + p[:, n * 128 : (n + 1) * 128]
                twist_acc[a, b, :] += total
                mg[a, b, :] = (g * wide(twist_t[a, b, :])).astype(BF16)

        loop(0, 8, unpack)

        def left_terms(blk):
            a, i = blk // 2, blk % 2
            b = pl.ds(pl.multiple_of(i * 256, 256), 256)
            left_acc[b, :] += dot_nt(mg[a, b, :], gated[cc, a])

        loop(0, 8, left_terms)

        def back(blk):
            a, i = blk // 2, blk % 2
            r = pl.multiple_of(blk * 256, 256)
            g = dot(left_t[pl.ds(pl.multiple_of(i * 256, 256), 256), :], mg[a])
            gk[par, pl.ds(r, 256), :] = g * conv(xv, cc, r, 256, 2)
            gv[par, pl.ds(r, 256), :] = g * conv(xk, cc, r, 256, 1)

        loop(0, 8, back)

        @pl.when(jnp.logical_not(first))
        def _():
            after_rows(cc, 0, gk).start()
            after_rows(cc, 1, gv).start()

    def conv_back(grad, par, ref, cc, stream, put, lo=0, hi=CC, write=True, count=True):
        span = hi - lo

        def step(blk, sums):
            r = pl.multiple_of(blk * 128, 128)
            g = grad[par, pl.ds(r, 136), lo:hi]
            if write:
                obuf[stream, pl.ds(r, 128), lo:hi] = (
                    tap(stream, 0, cc, lo, hi) * g[:128]
                    + tap(stream, 1, cc, lo, hi) * g[1:129]
                    + tap(stream, 2, cc, lo, hi) * g[2:130]
                ).astype(BF16)
            if count:
                shifted = shifts(ref, cc, r, 128, lo, hi)
                sums = tuple(sums[j] + jnp.sum((g[:128] * shifted[j]).reshape(16, 8, span), axis=0) for j in range(3))
            return sums

        sums = lax.fori_loop(0, 16, step, tuple(jnp.zeros((8, span), F32) for _ in range(3)))
        if count:
            for j in range(3):
                total = jnp.sum(sums[j], axis=0, keepdims=True)
                for n in range(span // 128):
                    put(cc * LANES + lo // 128 + n, j, total[:, n * 128 : (n + 1) * 128])

    outs = (q_out, k_out, v_out)

    def store(stream, cc, half=None):
        if half is None:
            return local(obuf.at[stream], outs[stream].at[:, lane(cc)], out_sem.at[stream, cc])
        return local(obuf.at[stream, :, pl.ds(half * 128, 128)], outs[stream].at[:, pl.ds(cc * CC + half * 128, 128)],
                     out_sem.at[stream, cc + half])

    def put_kv(base):
        def put(tile, j, value):
            ckv[tile, base + j : base + j + 1, :] = value

        return put

    def put_q(tile, j, value):
        if tile == TILES - 1:
            cq_last[j : j + 1, :] = value
        else:
            cq[3 * tile + j : 3 * tile + j + 1, :] = value

    def finish(grad, par, ref, cc, stream, put):
        if cc:
            store(stream, cc - 1).wait()
        conv_back(grad, par, ref, cc, stream, put)
        store(stream, cc).start()

    def kv_second(cc):
        par = cc % 2

        @pl.when(jnp.logical_not(last))
        def _():
            after_rows(cc, 0, gk).wait_recv()
            after_rows(cc, 1, gv).wait_recv()

        @pl.when(jnp.logical_not(first))
        def _():
            after_rows(cc, 0, gk).wait_send()
            after_rows(cc, 1, gv).wait_send()

        gk[par, TOKENS : TOKENS + 8, :] = kh[cc, 0]
        gv[par, TOKENS : TOKENS + 8, :] = kh[cc, 1]
        finish(gk, par, xk, cc, 1, put_kv(0))
        finish(gv, par, xv, cc, 2, put_kv(3))

    def monarch(cc):
        arrived(2, sr, cc)

        def put_sd(g, value):
            sd[:, pl.ds(pl.multiple_of(g * 32, 32), 32), :] = value

        spread(sr, cc, put_sd)

        def mul(b):
            zb[b] = dot(right[...], sd[b]).astype(BF16)
            right_acc[...] += dot_nt(gd[cc, b], sd[b])

        loop(0, 8, mul)
        gather_back(sr, cc)

    low, high = pl.ds(0, 128), pl.ds(128, 128)

    def send_monarch(cc):
        exchange(3, sr, mr, cc, low if cc == NC - 1 else slice(None))

        @pl.when(first)
        def _():
            def also(t):
                remote(sr.at[cc, t + 1, pl.ds(0, 16)], mh.at[cc], mh_s.at[cc], mh_r.at[cc], (d, t)).start()

            loop(1, SEQ - 1, also)
            local(sr.at[cc, 1, pl.ds(0, 16)], mh.at[cc], mh_r.at[cc]).start()

    partner = s + 1 - 2 * core

    def pair_copy():
        return remote(left_acc.at[pl.ds(pl.multiple_of((1 - core) * 256, 256), 256)], lx, l_s.at[0], l_r.at[0], (d, partner))

    def chip_of(i):
        t = (chip + i * 23) % 64
        return t, (t // 32, (t % 32) * 2 + core)

    def left_scatter():
        pair_copy().wait()
        half = left_acc[pl.ds(pl.multiple_of(core * 256, 256), 256), :] + lx[...]
        for n in range(4):
            lb[:, n] = half[:, n * 128 : (n + 1) * 128].astype(BF16).reshape(16, 16, 128)

        def send(i):
            t, dev = chip_of(i)
            remote(lb.at[t // 4, t % 4], li.at[chip], l_s.at[1], l_r.at[1], dev).start()

        loop(1, 64, send)
        local(lb.at[chip // 4, chip % 4], li.at[chip], l_r.at[1]).start()

    def left_gather():
        wait_bytes(li, l_r.at[1])
        lsum[...] = jnp.sum(li[...].astype(F32), axis=0).astype(BF16)

        def send(i):
            t, dev = chip_of(i)
            remote(lsum, lg.at[chip], l_s.at[2], l_r.at[2], dev).start()

        loop(1, 64, send)
        local(lsum, lg.at[chip], l_r.at[2]).start()

    def left_pair():
        return remote(lg, lg2, l_s.at[3], l_r.at[3], (d, partner))

    def left_finish():
        left_pair().wait()
        mine = lg[...].reshape(16, 4, 16, 128)
        other = lg2[...].reshape(16, 4, 16, 128)
        for n in range(4):
            left_out[pl.ds(pl.multiple_of(core * 256, 256), 256), n * 128 : (n + 1) * 128] = (
                mine[:, n].reshape(256, 128).astype(F32)
            )
            left_out[pl.ds(pl.multiple_of((1 - core) * 256, 256), 256), n * 128 : (n + 1) * 128] = (
                other[:, n].reshape(256, 128).astype(F32)
            )

    def right_pair_copies():
        return (
            remote(right_acc.at[pl.ds(pl.multiple_of((1 - core) * 128, 128), 128)], rx, r_s.at[0], r_r.at[0], (d, partner)),
            remote(ckv, kx, c_s, c_r, (d, partner)),
        )

    def right_scatter():
        for copy in right_pair_copies():
            copy.wait()
        rx[...] += right_acc[pl.ds(pl.multiple_of(core * 128, 128), 128), :]
        kx[...] += ckv[...]
        for n in range(2):
            for m in range(32):
                rb[n * 32 + m, 0:4, :] = rx[m * 4 : m * 4 + 4, n * 128 : (n + 1) * 128]
        for t in range(TILES):
            for j in range(6):
                rb[t * 6 + j, 4:5, :] = kx[t, j : j + 1, :]

        def send(i):
            t, dev = chip_of(i)
            remote(rb.at[t], ri.at[chip], r_s.at[1], r_r.at[1], dev).start()

        loop(1, 64, send)
        local(rb.at[chip], ri.at[chip], r_r.at[1]).start()

    def right_gather():
        wait_bytes(ri, r_r.at[1])
        rsum[...] = jnp.sum(ri[...], axis=0)

        def send(i):
            t, dev = chip_of(i)
            remote(rsum, rg.at[chip], r_s.at[2], r_r.at[2], dev).start()

        loop(1, 64, send)
        local(rsum, rg.at[chip], r_r.at[2]).start()

    def right_pair():
        return remote(rg, rg2, r_s.at[3], r_r.at[3], (d, partner))

    def right_finish():
        right_pair().wait()
        low_half, high_half = (
            [jnp.where(core == n, rg[m, 0:4, :], rg2[m, 0:4, :]) for m in range(64)] for n in range(2)
        )
        for n in range(2):
            for m in range(32):
                right_out[m * 4 : m * 4 + 4, n * 128 : (n + 1) * 128] = low_half[n * 32 + m]
                right_out[128 + m * 4 : 132 + m * 4, n * 128 : (n + 1) * 128] = high_half[n * 32 + m]

    inner, outer = x * 2 + core, d * 8 + zh * 4 + y

    def inner_dev(n):
        return d, (((n // 2) * 2 + zh) * 4 + y) * 2 + n % 2

    def outer_dev(n):
        return n // 8, ((x * 2 + (n // 4) % 2) * 4 + n % 4) * 2 + core

    def group_send(src, inbox, mine, n, dev_of, sem):
        def send(i):
            t = (mine + i) % n
            remote(src, inbox.at[mine], q_s.at[sem], q_r.at[sem], dev_of(t)).start()

        loop(1, n, send)
        inbox[mine] = src[...]

    def group_total(inbox, n, sem):
        wait_bytes(inbox.at[pl.ds(0, n - 1)], q_r.at[sem])
        return jnp.sum(inbox[...], axis=0)

    def group_sent(inbox, n, sem):
        wait_bytes(inbox.at[pl.ds(0, n - 1)], q_s.at[sem])

    kv_first(0)
    kv_first(1)
    kv_second(0)
    kv_first(2)
    pair_copy().start()
    for a in range(ROWS):
        tws[a : a + 1, :] = jnp.sum(jnp.transpose(twist_acc[a]), axis=0, keepdims=True)
    twist_copy = remote(tws, twx, tw_s, tw_r, (1 - d, s))
    twist_copy.start()
    left_scatter()
    monarch(0)
    send_monarch(0)
    kv_second(1)
    monarch(1)
    send_monarch(1)
    kv_second(2)
    monarch(2)
    for copy in right_pair_copies():
        copy.start()
    send_monarch(2)
    right_scatter()
    left_gather()

    def query_first(cc, lo, hi):
        par = cc % 2

        def unpack(blk):
            h, i = blk // 4, blk % 4
            m = mr[cc, pl.ds(i * 16, 16), pl.ds(pl.multiple_of(h * 16, 16), 16), lo:hi].astype(F32)
            for e in range(2):
                r = pl.multiple_of((2 * h + e) * COLS + i * 128, 128)
                gk[par, pl.ds(r, 128), lo:hi] = (
                    xo[cc, pl.ds(r, 128), lo:hi].astype(F32) * m[:, 8 * e : 8 * e + 8].reshape(128, hi - lo)
                )

        loop(0, 8, unpack)
        tail = xo[cc, TOKENS:WHOLE, lo:hi].astype(F32) * mh[cc, :, lo:hi].astype(F32)
        gk[par, TOKENS : TOKENS + 8, lo:hi] = tail[:8]

    def after_wait(cc):
        halo_wait(1, cc)

        @pl.when(jnp.logical_not(last))
        def _():
            wait_bytes(mh.at[cc], mh_r.at[cc])

    def query(cc):
        arrived(3, mr, cc)
        after_wait(cc)
        query_first(cc, 0, CC)
        finish(gk, cc % 2, xq, cc, 0, put_q)

    END = NC - 1
    exchange(4, sr, mr, END, high)
    query(0)
    query(1)
    right_gather()
    wait_bytes(lg, l_r.at[2])
    left_pair().start()
    twist_copy.wait()
    twist_out[...] = (tws[0:ROWS, :] + twx[0:ROWS, :]) / twist[...]
    store(0, END - 1).wait()
    arrived(3, mr, END, low)
    after_wait(END)
    query_first(END, 0, 128)
    conv_back(gk, END % 2, xq, END, 0, put_q, 0, 128)
    store(0, END, 0).start()
    group_send(cq, ia, inner, 8, inner_dev, 0)
    left_finish()
    arrived(4, mr, END, high)
    query_first(END, 128, 256)
    conv_back(gk, END % 2, xq, END, 0, put_q, 128, 256, write=False)
    group_send(cq_last, ia_last, inner, 8, inner_dev, 1)
    sb[...] = group_total(ia, 8, 0)
    group_send(sb, ib, outer, 16, outer_dev, 2)
    conv_back(gk, END % 2, xq, END, 0, put_q, 128, 256, count=False)
    wait_bytes(rg, r_r.at[2])
    right_pair().start()
    store(0, END, 1).start()
    sb_last[...] = group_total(ia_last, 8, 1)
    group_send(sb_last, ib_last, outer, 16, outer_dev, 3)
    right_finish()
    for t in range(TILES):
        lanes = slice(t * 128, (t + 1) * 128)
        for j in range(3):
            conv_out[1, j : j + 1, lanes] = rg[t * 6 + j, 4:5, :]
            conv_out[2, j : j + 1, lanes] = rg[t * 6 + 3 + j, 4:5, :]
    total = group_total(ib, 16, 2)
    for t in range(TILES - 1):
        conv_out[0, :, t * 128 : (t + 1) * 128] = total[3 * t : 3 * t + 3, :]
    conv_out[0, :, (TILES - 1) * 128 :] = group_total(ib_last, 16, 3)[0:3, :]

    for stream in (1, 2):
        store(stream, END).wait()
    store(0, END, 0).wait()
    store(0, END, 1).wait()
    for phase, src in enumerate((gs, gr, ss, sr, sr)):
        for cc in range(NC) if phase < 4 else (END,):
            lanes = slice(None)
            if phase >= 3 and cc == END:
                lanes = low if phase == 3 else high
            wait_bytes(src.at[cc, pl.ds(0, SEQ - 1), :, lanes], a2a_s.at[phase, cc])

    @pl.when(jnp.logical_not(last))
    def _():
        for n in (0, 2, 3):
            for cc in range(NC):
                halo(n, cc).wait_send()

    @pl.when(jnp.logical_not(first))
    def _():
        for cc in range(NC):
            halo(1, cc).wait_send()

    @pl.when(first)
    def _():
        for cc in range(NC):
            wait_bytes(sr.at[cc, pl.ds(0, SEQ - 2), pl.ds(0, 16)], mh_s.at[cc])

    wait_bytes(li.at[pl.ds(0, 63)], l_s.at[1])
    wait_bytes(li.at[pl.ds(0, 63)], l_s.at[2])
    wait_bytes(ri.at[pl.ds(0, 63)], r_s.at[1])
    wait_bytes(ri.at[pl.ds(0, 63)], r_s.at[2])
    for box, n, sem in ((ia, 8, 0), (ia_last, 8, 1), (ib, 16, 2), (ib_last, 16, 3)):
        group_sent(box, n, sem)


def vmem(*shape, dtype=BF16):
    return pltpu.VMEM(shape, dtype)


def dma(*shape):
    return pltpu.SemaphoreType.DMA(shape)


PIECES = 8


def write_out(*refs):
    ins, outs, through, (enter, leave) = refs[:7], refs[7:14], refs[14:21], refs[21:]
    n_rows = TOKENS // PIECES
    parts = [(n, p, pl.ds(p * n_rows, n_rows)) for p in range(PIECES) for n in range(3)]
    parts += [(n, 0, slice(None)) for n in range(3, 7)]
    first = [pltpu.make_async_copy(ins[n].at[r], through[n].at[r], enter.at[n, p]) for n, p, r in parts]
    second = [pltpu.make_async_copy(through[n].at[r], outs[n].at[r], leave.at[n, p]) for n, p, r in parts]
    for copy in first:
        copy.start()
    for copy, on in zip(first, second):
        copy.wait()
        on.start()
    for copy in second:
        copy.wait()


def shards(query_raw, key_raw, value_raw, out_grad, conv_taps, left_block, right_block, twiddle):
    flat = [a.reshape(TOKENS, CH) for a in (query_raw, key_raw, value_raw, out_grad)]
    anywhere, inside = pl.BlockSpec(memory_space=pl.ANY), pl.BlockSpec(memory_space=pltpu.VMEM)
    staged = vmem(NC, SEQ, 32, CC)
    scratch = (
        [vmem(NC, WHOLE, CC)] * 4
        + [staged] * 6
        + [vmem(NC, 8, 256, CC), vmem(NC, ROWS, COLS, CC), vmem(8, 256, CC), vmem(8, 256, CC), vmem(ROWS, COLS, CC)]
        + [vmem(2, TOKENS + 8, CC, dtype=F32)] * 2
        + [vmem(3, TOKENS, CC), vmem(NC, 16, CC), vmem(NC, 2, 8, CC, dtype=F32)]
        + [vmem(256, 256), vmem(256, 256), vmem(COLS, COLS), vmem(256, 256)]
        + [vmem(ROWS, COLS, 128, dtype=F32)] * 2
        + [vmem(8, COLS, dtype=F32)] * 2
        + [vmem(COLS, COLS, dtype=F32), vmem(256, 256, dtype=F32), vmem(256, COLS, dtype=F32)]
        + [vmem(16, 4, 16, 128), vmem(64, 16, 128), vmem(16, 128), vmem(64, 16, 128), vmem(64, 16, 128)]
        + [vmem(128, 256, dtype=F32), vmem(TILES, 8, 128, dtype=F32), vmem(64, 8, 128, dtype=F32), vmem(64, 8, 128, dtype=F32)]
        + [vmem(8, 128, dtype=F32), vmem(64, 8, 128, dtype=F32), vmem(64, 8, 128, dtype=F32)]
        + [vmem(TILES, 8, 128, dtype=F32), vmem(16, 128, dtype=F32), vmem(8, 128, dtype=F32)]
        + [vmem(8, 16, 128, dtype=F32), vmem(8, 8, 128, dtype=F32), vmem(16, 16, 128, dtype=F32), vmem(16, 8, 128, dtype=F32)]
        + [vmem(16, 128, dtype=F32), vmem(8, 128, dtype=F32)]
        + [dma(4, NC), dma(4, NC), dma(4, NC), dma(5, NC), dma(5, NC), dma(NC), dma(NC), dma(NC, 2), dma(NC, 2), dma(3, NC + 1)]
        + [dma(4), dma(4), dma(4), dma(4), dma(), dma(), dma(), dma(), dma(4), dma(4)]
    )
    results = pl.pallas_call(
        kernel,
        name="monarch_back",
        out_shape=[
            jax.ShapeDtypeStruct((TOKENS, CH), BF16),
            jax.ShapeDtypeStruct((TOKENS, CH), BF16),
            jax.ShapeDtypeStruct((TOKENS, CH), BF16),
            jax.ShapeDtypeStruct((3, 3, CH), F32),
            jax.ShapeDtypeStruct((COLS, COLS), F32),
            jax.ShapeDtypeStruct((256, 256), F32),
            jax.ShapeDtypeStruct((ROWS, COLS), F32),
        ],
        in_specs=[anywhere] * 4 + [inside] * 4,
        out_specs=[anywhere] * 3 + [inside] * 4,
        scratch_shapes=scratch,
        compiler_params=pltpu.CompilerParams(
            collective_id=0, has_side_effects=True, vmem_limit_bytes=VMEM_LIMIT
        ),
    )(flat[0], flat[1], flat[2], flat[3], conv_taps, left_block, right_block, twiddle)
    results = pl.pallas_call(
        write_out,
        name="write_out",
        out_shape=[jax.ShapeDtypeStruct(r.shape, r.dtype) for r in results],
        in_specs=[pl.BlockSpec(memory_space=pltpu.HBM)] * 7,
        out_specs=[pl.BlockSpec(memory_space=pltpu.HBM)] * 7,
        scratch_shapes=[pltpu.VMEM(r.shape, r.dtype) for r in results] + [dma(7, PIECES)] * 2,
        compiler_params=pltpu.CompilerParams(vmem_limit_bytes=VMEM_LIMIT),
    )(*results)
    return tuple(r.reshape(1, TOKENS, CH) for r in results[:3]) + tuple(results[3:])


def solution(mesh):
    rows = P("dp", "seq", None)
    return jax.shard_map(
        shards,
        mesh=mesh,
        in_specs=(rows, rows, rows, rows, P(), P(), P(), P("seq", None)),
        out_specs=(rows, rows, rows, P(), P(), P(), P("seq", None)),
        check_vma=False,
    )
```

```python
import jax
import jax.numpy as jnp
from jax import lax
from jax.experimental import pallas as pl
from jax.experimental.pallas import tpu as pltpu
from jax.sharding import PartitionSpec as P

F32, BF16 = jnp.float32, jnp.bfloat16
MESH = pl.DeviceIdType.MESH
SEQ, DP = 64, 2
DEVICES = SEQ * DP
ROWS, COLS, CH = 4, 512, 768
TOKENS = ROWS * COLS
CC = 256
NC = CH // CC
LANES = CC // 128
TILES = CH // 128
WHOLE = TOKENS + 16
VMEM_LIMIT = 62 * 2**20


def dot(a, b):
    return jnp.dot(a, b, preferred_element_type=F32)


def dot_nt(a, b):
    return lax.dot_general(a, b, (((1,), (1,)), ((), ())), preferred_element_type=F32)


def loop(lo, hi, body):
    def step(i, carry):
        body(i)
        return carry

    lax.fori_loop(lo, hi, step, 0)


def wide(column):
    return jnp.concatenate([column] * LANES, axis=1)


def kernel(
    q_in, k_in, v_in, o_in, taps, left, right, twist,
    q_out, k_out, v_out, conv_out, left_out, right_out, twist_out,
    xq, xk, xv, xo, gs, gr, br, ss, sr, mr, gd, gated, sd, zb, mg, gk, gv,
    obuf, mh, kh, perm, perm_t, left_t, right_t, twist_t, twist_acc, tws, twx,
    left_acc, right_acc, lx, lb, li, lsum, lg, lg2, rx, kx, rb, ri, rsum, rg, rg2,
    ckv, cq, cq_last, ia, ia_last, ib, ib_last, sb, sb_last,
    in_sem, halo_s, halo_r, a2a_s, a2a_r, mh_s, mh_r, kh_s, kh_r, out_sem,
    l_s, l_r, r_s, r_r, c_s, c_r, tw_s, tw_r, q_s, q_r,
):
    d, s = lax.axis_index("dp"), lax.axis_index("seq")
    x, zh, y, core = s // 16, (s // 8) % 2, (s // 2) % 4, s % 2
    me = d * SEQ + s
    chip = d * 32 + s // 2
    first, last = s == 0, s == SEQ - 1

    def peer(i):
        o = (i * 9) % 64
        bit = [(o // (1 << n)) % 2 for n in range(6)]
        dx, dz, dy, dc = 2 * bit[0] + bit[2], bit[1], 2 * bit[3] + bit[4], bit[5]
        dx = dx + core * (4 - 2 * dx)
        dy = dy + core * (4 - 2 * dy)
        return (((x + dx) % 4 * 2 + (zh + dz) % 2) * 4 + (y + dy) % 4) * 2 + (core + dc) % 2

    def local(src, dst, sem):
        return pltpu.make_async_copy(src, dst, sem)

    def remote(src, dst, ssem, rsem, dev):
        return pltpu.make_async_remote_copy(
            src_ref=src, dst_ref=dst, send_sem=ssem, recv_sem=rsem, device_id=dev, device_id_type=MESH
        )

    def wait_bytes(ref, sem):
        pltpu.make_async_copy(ref, ref, sem).wait()

    def lane(cc):
        return pl.ds(cc * CC, CC)

    barrier = pltpu.get_barrier_semaphore()

    def greet(i):
        t = (me + i) % DEVICES
        pl.semaphore_signal(barrier, inc=1, device_id=(t // SEQ, t % SEQ), device_id_type=MESH)

    loop(1, DEVICES, greet)

    ins = (q_in, o_in, k_in, v_in)
    bufs = (xq, xo, xk, xv)

    def load(n, cc):
        row = 0 if n == 1 else 16
        return local(ins[n].at[:, lane(cc)], bufs[n].at[cc, pl.ds(row, TOKENS)], in_sem.at[n, cc])

    for pair in ((0, 1), (2, 3)):
        for cc in range(NC):
            for n in pair:
                load(n, cc).start()

    def halo(n, cc):
        if n == 1:
            return remote(o_in.at[pl.ds(0, 16), lane(cc)], xo.at[cc, pl.ds(TOKENS, 16)],
                          halo_s.at[n, cc], halo_r.at[n, cc], (d, jnp.maximum(s - 1, 0)))
        return remote(ins[n].at[pl.ds(TOKENS - 16, 16), lane(cc)], bufs[n].at[cc, pl.ds(0, 16)],
                      halo_s.at[n, cc], halo_r.at[n, cc], (d, jnp.minimum(s + 1, SEQ - 1)))

    @pl.when(first)
    def _():
        for ref in (xq, xk, xv):
            ref[:, 0:16, :] = jnp.zeros((NC, 16, CC), BF16)

    @pl.when(last)
    def _():
        xo[:, TOKENS:WHOLE, :] = jnp.zeros((NC, 16, CC), BF16)
        mh[...] = jnp.zeros_like(mh)
        kh[...] = jnp.zeros_like(kh)

    def tap(stream, j, cc, lo=0, hi=CC):
        return taps[stream, j : j + 1, cc * CC + lo : cc * CC + hi]

    def shifts(ref, cc, r, n, lo=0, hi=CC):
        wide_x = ref[cc, pl.ds(r, n + 16), lo:hi].astype(F32)
        return wide_x[16:], wide_x[15:-1], wide_x[14:-2]

    def conv(ref, cc, r, n, stream):
        x0, x1, x2 = shifts(ref, cc, r, n)
        return tap(stream, 0, cc) * x0 + tap(stream, 1, cc) * x1 + tap(stream, 2, cc) * x2

    def gate_block(cc, blk):
        h, i = blk // 4, blk % 4
        parts = []
        for e in range(2):
            r = pl.multiple_of((2 * h + e) * COLS + i * 128, 128)
            g = xo[cc, pl.ds(r, 128), :].astype(F32) * conv(xq, cc, r, 128, 0)
            parts.append(g.reshape(16, 8, CC))
        gs[cc, pl.ds(i * 16, 16), pl.ds(pl.multiple_of(h * 16, 16), 16), :] = jnp.concatenate(parts, 1).astype(BF16)

    def exchange(phase, src, dst, cc, lanes=slice(None)):
        def part(ref, t):
            return ref.at[cc, t, :, lanes]

        def send(i):
            t = peer(i)
            remote(part(src, t), part(dst, s), a2a_s.at[phase, cc], a2a_r.at[phase, cc], (d, t)).start()

        loop(1, SEQ, send)
        local(part(src, s), part(dst, s), a2a_r.at[phase, cc]).start()

    def arrived(phase, dst, cc, lanes=slice(None)):
        wait_bytes(dst.at[cc, :, :, lanes], a2a_r.at[phase, cc])

    def halo_wait(n, cc):
        @pl.when(jnp.logical_not(last if n == 1 else first))
        def _():
            halo(n, cc).wait_recv()

    load(0, 0).wait()
    load(1, 0).wait()
    loop(0, 7, lambda n: gate_block(0, 7 - n))
    pl.semaphore_wait(barrier, DEVICES - 1)
    for n in (0, 2, 3):
        @pl.when(jnp.logical_not(last))
        def _():
            for cc in range(NC):
                halo(n, cc).start()

    @pl.when(jnp.logical_not(first))
    def _():
        for cc in range(NC):
            halo(1, cc).start()

    halo_wait(0, 0)
    gate_block(0, 0)
    exchange(0, gs, gr, 0)
    for cc in range(1, NC):
        load(0, cc).wait()
        load(1, cc).wait()
        halo_wait(0, cc)
        loop(0, 8, lambda n: gate_block(cc, n))
        exchange(0, gs, gr, cc)

    row = lax.broadcasted_iota(jnp.int32, (256, 256), 0)
    col = lax.broadcasted_iota(jnp.int32, (256, 256), 1)
    perm[...] = jnp.where(col == (row & 31) * 8 + (row >> 5), 1.0, 0.0).astype(BF16)
    perm_t[...] = jnp.where(row == (col & 31) * 8 + (col >> 5), 1.0, 0.0).astype(BF16)
    left_t[...] = jnp.transpose(left[...].astype(F32)).astype(BF16)
    right_t[...] = jnp.transpose(right[...].astype(F32)).astype(BF16)
    for a in range(ROWS):
        twist_t[a] = jnp.transpose(jnp.broadcast_to(twist[a : a + 1, :], (128, COLS)))
    twist_acc[...] = jnp.zeros_like(twist_acc)
    left_acc[...] = jnp.zeros_like(left_acc)
    right_acc[...] = jnp.zeros_like(right_acc)
    ckv[...] = jnp.zeros_like(ckv)
    cq[...] = jnp.zeros_like(cq)
    cq_last[...] = jnp.zeros_like(cq_last)
    tws[...] = jnp.zeros_like(tws)
    rb[...] = jnp.zeros_like(rb)

    def scaled(cc):
        def make_gated(blk):
            a, i = blk // 4, blk % 4
            r = pl.multiple_of(blk * 128, 128)
            gated[cc, a, pl.ds(pl.multiple_of(i * 128, 128), 128), :] = (
                conv(xk, cc, r, 128, 1) * conv(xv, cc, r, 128, 2)
            ).astype(BF16)

        loop(0, 16, make_gated)

        def mix(blk):
            h, i = blk // 2, blk % 2
            b = pl.ds(pl.multiple_of(i * 256, 256), 256)
            parts = []
            for e in range(2):
                m = dot(left[b, :], gated[cc, 2 * h + e]) * wide(twist_t[2 * h + e, b, :])
                parts.append(m.reshape(32, 8, CC))
            ss[cc, pl.ds(i * 32, 32), pl.ds(pl.multiple_of(h * 16, 16), 16), :] = jnp.concatenate(parts, 1).astype(BF16)

        loop(0, 4, mix)

    for cc in range(NC):
        for n in (2, 3):
            load(n, cc).wait()
            halo_wait(n, cc)
        scaled(cc)

    def spread(src, cc, put):
        def go(g):
            block = src[cc, pl.ds(g * 8, 8), :, :].reshape(256, CC)
            put(g, dot(perm[...], block).astype(BF16).reshape(8, 32, CC))

        loop(0, 8, go)

    def gather_back(dst, cc):
        def go(g):
            block = zb[:, pl.ds(pl.multiple_of(g * 32, 32), 32), :].reshape(256, CC)
            dst[cc, pl.ds(g * 8, 8), :, :] = dot(perm_t[...], block).astype(BF16).reshape(8, 32, CC)

        loop(0, 8, go)

    for cc in range(NC):
        arrived(0, gr, cc)

        def put_gd(g, value):
            gd[cc, :, pl.ds(pl.multiple_of(g * 32, 32), 32), :] = value

        spread(gr, cc, put_gd)

        def back_mul(b):
            zb[b] = dot(right_t[...], gd[cc, b]).astype(BF16)

        loop(0, 8, back_mul)
        gather_back(gr, cc)
        exchange(1, gr, br, cc)
    for cc in range(NC):
        exchange(2, ss, sr, cc)

    def after_rows(cc, stream, which):
        return remote(which.at[cc % 2, pl.ds(0, 8)], kh.at[cc, stream], kh_s.at[cc, stream], kh_r.at[cc, stream],
                      (d, jnp.maximum(s - 1, 0)))

    def kv_first(cc):
        par = cc % 2
        arrived(1, br, cc)

        def unpack(blk):
            h, i = blk // 4, blk % 4
            peers, half = pl.ds(i * 16, 16), pl.ds(pl.multiple_of(h * 16, 16), 16)
            b = pl.ds(pl.multiple_of(i * 128, 128), 128)
            grads, products = br[cc, peers, half, :].astype(F32), ss[cc, peers, half, :].astype(F32)
            for e in range(2):
                a = 2 * h + e
                g = grads[:, 8 * e : 8 * e + 8].reshape(128, CC)
                p = g * products[:, 8 * e : 8 * e + 8].reshape(128, CC)
                total = p[:, :128]
                for n in range(1, LANES):
                    total = total + p[:, n * 128 : (n + 1) * 128]
                twist_acc[a, b, :] += total
                mg[a, b, :] = (g * wide(twist_t[a, b, :])).astype(BF16)

        loop(0, 8, unpack)

        def left_terms(blk):
            a, i = blk // 2, blk % 2
            b = pl.ds(pl.multiple_of(i * 256, 256), 256)
            left_acc[b, :] += dot_nt(mg[a, b, :], gated[cc, a])

        loop(0, 8, left_terms)

        def back(blk):
            a, i = blk // 2, blk % 2
            r = pl.multiple_of(blk * 256, 256)
            g = dot(left_t[pl.ds(pl.multiple_of(i * 256, 256), 256), :], mg[a])
            gk[par, pl.ds(r, 256), :] = g * conv(xv, cc, r, 256, 2)
            gv[par, pl.ds(r, 256), :] = g * conv(xk, cc, r, 256, 1)

        loop(0, 8, back)

        @pl.when(jnp.logical_not(first))
        def _():
            after_rows(cc, 0, gk).start()
            after_rows(cc, 1, gv).start()

    def conv_back(grad, par, ref, cc, stream, put, lo=0, hi=CC, write=True, count=True):
        span = hi - lo

        def step(blk, sums):
            r = pl.multiple_of(blk * 128, 128)
            g = grad[par, pl.ds(r, 136), lo:hi]
            if write:
                obuf[stream, pl.ds(r, 128), lo:hi] = (
                    tap(stream, 0, cc, lo, hi) * g[:128]
                    + tap(stream, 1, cc, lo, hi) * g[1:129]
                    + tap(stream, 2, cc, lo, hi) * g[2:130]
                ).astype(BF16)
            if count:
                shifted = shifts(ref, cc, r, 128, lo, hi)
                sums = tuple(sums[j] + jnp.sum((g[:128] * shifted[j]).reshape(16, 8, span), axis=0) for j in range(3))
            return sums

        sums = lax.fori_loop(0, 16, step, tuple(jnp.zeros((8, span), F32) for _ in range(3)))
        if count:
            for j in range(3):
                total = jnp.sum(sums[j], axis=0, keepdims=True)
                for n in range(span // 128):
                    put(cc * LANES + lo // 128 + n, j, total[:, n * 128 : (n + 1) * 128])

    outs = (q_out, k_out, v_out)

    def store(stream, cc, half=None):
        if half is None:
            return local(obuf.at[stream], outs[stream].at[:, lane(cc)], out_sem.at[stream, cc])
        return local(obuf.at[stream, :, pl.ds(half * 128, 128)], outs[stream].at[:, pl.ds(cc * CC + half * 128, 128)],
                     out_sem.at[stream, cc + half])

    def put_kv(base):
        def put(tile, j, value):
            ckv[tile, base + j : base + j + 1, :] = value

        return put

    def put_q(tile, j, value):
        if tile == TILES - 1:
            cq_last[j : j + 1, :] = value
        else:
            cq[3 * tile + j : 3 * tile + j + 1, :] = value

    def finish(grad, par, ref, cc, stream, put):
        if cc:
            store(stream, cc - 1).wait()
        conv_back(grad, par, ref, cc, stream, put)
        store(stream, cc).start()

    def kv_second(cc):
        par = cc % 2

        @pl.when(jnp.logical_not(last))
        def _():
            after_rows(cc, 0, gk).wait_recv()
            after_rows(cc, 1, gv).wait_recv()

        @pl.when(jnp.logical_not(first))
        def _():
            after_rows(cc, 0, gk).wait_send()
            after_rows(cc, 1, gv).wait_send()

        gk[par, TOKENS : TOKENS + 8, :] = kh[cc, 0]
        gv[par, TOKENS : TOKENS + 8, :] = kh[cc, 1]
        finish(gk, par, xk, cc, 1, put_kv(0))
        finish(gv, par, xv, cc, 2, put_kv(3))

    def monarch(cc):
        arrived(2, sr, cc)

        def put_sd(g, value):
            sd[:, pl.ds(pl.multiple_of(g * 32, 32), 32), :] = value

        spread(sr, cc, put_sd)

        def mul(b):
            zb[b] = dot(right[...], sd[b]).astype(BF16)
            right_acc[...] += dot_nt(gd[cc, b], sd[b])

        loop(0, 8, mul)
        gather_back(sr, cc)

    low, high = pl.ds(0, 128), pl.ds(128, 128)

    def send_monarch(cc):
        exchange(3, sr, mr, cc, low if cc == NC - 1 else slice(None))

        @pl.when(first)
        def _():
            def also(t):
                remote(sr.at[cc, t + 1, pl.ds(0, 16)], mh.at[cc], mh_s.at[cc], mh_r.at[cc], (d, t)).start()

            loop(1, SEQ - 1, also)
            local(sr.at[cc, 1, pl.ds(0, 16)], mh.at[cc], mh_r.at[cc]).start()

    partner = s + 1 - 2 * core

    def pair_copy():
        return remote(left_acc.at[pl.ds(pl.multiple_of((1 - core) * 256, 256), 256)], lx, l_s.at[0], l_r.at[0], (d, partner))

    def chip_of(i):
        t = (chip + i * 23) % 64
        return t, (t // 32, (t % 32) * 2 + core)

    def left_scatter():
        pair_copy().wait()
        half = left_acc[pl.ds(pl.multiple_of(core * 256, 256), 256), :] + lx[...]
        for n in range(4):
            lb[:, n] = half[:, n * 128 : (n + 1) * 128].astype(BF16).reshape(16, 16, 128)

        def send(i):
            t, dev = chip_of(i)
            remote(lb.at[t // 4, t % 4], li.at[chip], l_s.at[1], l_r.at[1], dev).start()

        loop(1, 64, send)
        local(lb.at[chip // 4, chip % 4], li.at[chip], l_r.at[1]).start()

    def left_gather():
        wait_bytes(li, l_r.at[1])
        lsum[...] = jnp.sum(li[...].astype(F32), axis=0).astype(BF16)

        def send(i):
            t, dev = chip_of(i)
            remote(lsum, lg.at[chip], l_s.at[2], l_r.at[2], dev).start()

        loop(1, 64, send)
        local(lsum, lg.at[chip], l_r.at[2]).start()

    def left_pair():
        return remote(lg, lg2, l_s.at[3], l_r.at[3], (d, partner))

    def left_finish():
        left_pair().wait()
        mine = lg[...].reshape(16, 4, 16, 128)
        other = lg2[...].reshape(16, 4, 16, 128)
        for n in range(4):
            left_out[pl.ds(pl.multiple_of(core * 256, 256), 256), n * 128 : (n + 1) * 128] = (
                mine[:, n].reshape(256, 128).astype(F32)
            )
            left_out[pl.ds(pl.multiple_of((1 - core) * 256, 256), 256), n * 128 : (n + 1) * 128] = (
                other[:, n].reshape(256, 128).astype(F32)
            )

    def right_pair_copies():
        return (
            remote(right_acc.at[pl.ds(pl.multiple_of((1 - core) * 128, 128), 128)], rx, r_s.at[0], r_r.at[0], (d, partner)),
            remote(ckv, kx, c_s, c_r, (d, partner)),
        )

    def right_scatter():
        for copy in right_pair_copies():
            copy.wait()
        rx[...] += right_acc[pl.ds(pl.multiple_of(core * 128, 128), 128), :]
        kx[...] += ckv[...]
        for n in range(2):
            for m in range(32):
                rb[n * 32 + m, 0:4, :] = rx[m * 4 : m * 4 + 4, n * 128 : (n + 1) * 128]
        for t in range(TILES):
            for j in range(6):
                rb[t * 6 + j, 4:5, :] = kx[t, j : j + 1, :]

        def send(i):
            t, dev = chip_of(i)
            remote(rb.at[t], ri.at[chip], r_s.at[1], r_r.at[1], dev).start()

        loop(1, 64, send)
        local(rb.at[chip], ri.at[chip], r_r.at[1]).start()

    def right_gather():
        wait_bytes(ri, r_r.at[1])
        rsum[...] = jnp.sum(ri[...], axis=0)

        def send(i):
            t, dev = chip_of(i)
            remote(rsum, rg.at[chip], r_s.at[2], r_r.at[2], dev).start()

        loop(1, 64, send)
        local(rsum, rg.at[chip], r_r.at[2]).start()

    def right_pair():
        return remote(rg, rg2, r_s.at[3], r_r.at[3], (d, partner))

    def right_finish():
        right_pair().wait()
        low_half, high_half = (
            [jnp.where(core == n, rg[m, 0:4, :], rg2[m, 0:4, :]) for m in range(64)] for n in range(2)
        )
        for n in range(2):
            for m in range(32):
                right_out[m * 4 : m * 4 + 4, n * 128 : (n + 1) * 128] = low_half[n * 32 + m]
                right_out[128 + m * 4 : 132 + m * 4, n * 128 : (n + 1) * 128] = high_half[n * 32 + m]

    inner, outer = x * 2 + core, d * 8 + zh * 4 + y

    def inner_dev(n):
        return d, (((n // 2) * 2 + zh) * 4 + y) * 2 + n % 2

    def outer_dev(n):
        return n // 8, ((x * 2 + (n // 4) % 2) * 4 + n % 4) * 2 + core

    def group_send(src, inbox, mine, n, dev_of, sem):
        def send(i):
            t = (mine + i) % n
            remote(src, inbox.at[mine], q_s.at[sem], q_r.at[sem], dev_of(t)).start()

        loop(1, n, send)
        inbox[mine] = src[...]

    def group_total(inbox, n, sem):
        wait_bytes(inbox.at[pl.ds(0, n - 1)], q_r.at[sem])
        return jnp.sum(inbox[...], axis=0)

    def group_sent(inbox, n, sem):
        wait_bytes(inbox.at[pl.ds(0, n - 1)], q_s.at[sem])

    kv_first(0)
    kv_first(1)
    kv_second(0)
    kv_first(2)
    pair_copy().start()
    for a in range(ROWS):
        tws[a : a + 1, :] = jnp.sum(jnp.transpose(twist_acc[a]), axis=0, keepdims=True)
    twist_copy = remote(tws, twx, tw_s, tw_r, (1 - d, s))
    twist_copy.start()
    left_scatter()
    monarch(0)
    send_monarch(0)
    kv_second(1)
    monarch(1)
    send_monarch(1)
    kv_second(2)
    monarch(2)
    for copy in right_pair_copies():
        copy.start()
    send_monarch(2)
    right_scatter()
    left_gather()

    def query_first(cc, lo, hi):
        par = cc % 2

        def unpack(blk):
            h, i = blk // 4, blk % 4
            m = mr[cc, pl.ds(i * 16, 16), pl.ds(pl.multiple_of(h * 16, 16), 16), lo:hi].astype(F32)
            for e in range(2):
                r = pl.multiple_of((2 * h + e) * COLS + i * 128, 128)
                gk[par, pl.ds(r, 128), lo:hi] = (
                    xo[cc, pl.ds(r, 128), lo:hi].astype(F32) * m[:, 8 * e : 8 * e + 8].reshape(128, hi - lo)
                )

        loop(0, 8, unpack)
        tail = xo[cc, TOKENS:WHOLE, lo:hi].astype(F32) * mh[cc, :, lo:hi].astype(F32)
        gk[par, TOKENS : TOKENS + 8, lo:hi] = tail[:8]

    def after_wait(cc):
        halo_wait(1, cc)

        @pl.when(jnp.logical_not(last))
        def _():
            wait_bytes(mh.at[cc], mh_r.at[cc])

    def query(cc):
        arrived(3, mr, cc)
        after_wait(cc)
        query_first(cc, 0, CC)
        finish(gk, cc % 2, xq, cc, 0, put_q)

    END = NC - 1
    exchange(4, sr, mr, END, high)
    query(0)
    query(1)
    right_gather()
    wait_bytes(lg, l_r.at[2])
    left_pair().start()
    twist_copy.wait()
    twist_out[...] = (tws[0:ROWS, :] + twx[0:ROWS, :]) / twist[...]
    store(0, END - 1).wait()
    arrived(3, mr, END, low)
    after_wait(END)
    query_first(END, 0, 128)
    conv_back(gk, END % 2, xq, END, 0, put_q, 0, 128)
    store(0, END, 0).start()
    group_send(cq, ia, inner, 8, inner_dev, 0)
    left_finish()
    arrived(4, mr, END, high)
    query_first(END, 128, 256)
    conv_back(gk, END % 2, xq, END, 0, put_q, 128, 256, write=False)
    group_send(cq_last, ia_last, inner, 8, inner_dev, 1)
    sb[...] = group_total(ia, 8, 0)
    group_send(sb, ib, outer, 16, outer_dev, 2)
    conv_back(gk, END % 2, xq, END, 0, put_q, 128, 256, count=False)
    wait_bytes(rg, r_r.at[2])
    right_pair().start()
    store(0, END, 1).start()
    sb_last[...] = group_total(ia_last, 8, 1)
    group_send(sb_last, ib_last, outer, 16, outer_dev, 3)
    right_finish()
    for t in range(TILES):
        lanes = slice(t * 128, (t + 1) * 128)
        for j in range(3):
            conv_out[1, j : j + 1, lanes] = rg[t * 6 + j, 4:5, :]
            conv_out[2, j : j + 1, lanes] = rg[t * 6 + 3 + j, 4:5, :]
    total = group_total(ib, 16, 2)
    for t in range(TILES - 1):
        conv_out[0, :, t * 128 : (t + 1) * 128] = total[3 * t : 3 * t + 3, :]
    conv_out[0, :, (TILES - 1) * 128 :] = group_total(ib_last, 16, 3)[0:3, :]

    for stream in (1, 2):
        store(stream, END).wait()
    store(0, END, 0).wait()
    store(0, END, 1).wait()
    for phase, src in enumerate((gs, gr, ss, sr, sr)):
        for cc in range(NC) if phase < 4 else (END,):
            lanes = slice(None)
            if phase >= 3 and cc == END:
                lanes = low if phase == 3 else high
            wait_bytes(src.at[cc, pl.ds(0, SEQ - 1), :, lanes], a2a_s.at[phase, cc])

    @pl.when(jnp.logical_not(last))
    def _():
        for n in (0, 2, 3):
            for cc in range(NC):
                halo(n, cc).wait_send()

    @pl.when(jnp.logical_not(first))
    def _():
        for cc in range(NC):
            halo(1, cc).wait_send()

    @pl.when(first)
    def _():
        for cc in range(NC):
            wait_bytes(sr.at[cc, pl.ds(0, SEQ - 2), pl.ds(0, 16)], mh_s.at[cc])

    wait_bytes(li.at[pl.ds(0, 63)], l_s.at[1])
    wait_bytes(li.at[pl.ds(0, 63)], l_s.at[2])
    wait_bytes(ri.at[pl.ds(0, 63)], r_s.at[1])
    wait_bytes(ri.at[pl.ds(0, 63)], r_s.at[2])
    for box, n, sem in ((ia, 8, 0), (ia_last, 8, 1), (ib, 16, 2), (ib_last, 16, 3)):
        group_sent(box, n, sem)


def vmem(*shape, dtype=BF16):
    return pltpu.VMEM(shape, dtype)


def dma(*shape):
    return pltpu.SemaphoreType.DMA(shape)


PIECES = 16


def write_out(*refs):
    ins, outs, through, (enter, leave) = refs[:7], refs[7:14], refs[14:21], refs[21:]
    n_rows = TOKENS // PIECES
    parts = [(n, 0, slice(None)) for n in range(3, 7)]
    parts += [(n, p, pl.ds(p * n_rows, n_rows)) for p in range(PIECES) for n in range(3)]
    first = [pltpu.make_async_copy(ins[n].at[r], through[n].at[r], enter.at[n, p]) for n, p, r in parts]
    second = [pltpu.make_async_copy(through[n].at[r], outs[n].at[r], leave.at[n, p]) for n, p, r in parts]
    for copy in first:
        copy.start()
    for copy, on in zip(first, second):
        copy.wait()
        on.start()
    for copy in second:
        copy.wait()


def shards(query_raw, key_raw, value_raw, out_grad, conv_taps, left_block, right_block, twiddle):
    flat = [a.reshape(TOKENS, CH) for a in (query_raw, key_raw, value_raw, out_grad)]
    anywhere, inside = pl.BlockSpec(memory_space=pl.ANY), pl.BlockSpec(memory_space=pltpu.VMEM)
    staged = vmem(NC, SEQ, 32, CC)
    scratch = (
        [vmem(NC, WHOLE, CC)] * 4
        + [staged] * 6
        + [vmem(NC, 8, 256, CC), vmem(NC, ROWS, COLS, CC), vmem(8, 256, CC), vmem(8, 256, CC), vmem(ROWS, COLS, CC)]
        + [vmem(2, TOKENS + 8, CC, dtype=F32)] * 2
        + [vmem(3, TOKENS, CC), vmem(NC, 16, CC), vmem(NC, 2, 8, CC, dtype=F32)]
        + [vmem(256, 256), vmem(256, 256), vmem(COLS, COLS), vmem(256, 256)]
        + [vmem(ROWS, COLS, 128, dtype=F32)] * 2
        + [vmem(8, COLS, dtype=F32)] * 2
        + [vmem(COLS, COLS, dtype=F32), vmem(256, 256, dtype=F32), vmem(256, COLS, dtype=F32)]
        + [vmem(16, 4, 16, 128), vmem(64, 16, 128), vmem(16, 128), vmem(64, 16, 128), vmem(64, 16, 128)]
        + [vmem(128, 256, dtype=F32), vmem(TILES, 8, 128, dtype=F32), vmem(64, 8, 128, dtype=F32), vmem(64, 8, 128, dtype=F32)]
        + [vmem(8, 128, dtype=F32), vmem(64, 8, 128, dtype=F32), vmem(64, 8, 128, dtype=F32)]
        + [vmem(TILES, 8, 128, dtype=F32), vmem(16, 128, dtype=F32), vmem(8, 128, dtype=F32)]
        + [vmem(8, 16, 128, dtype=F32), vmem(8, 8, 128, dtype=F32), vmem(16, 16, 128, dtype=F32), vmem(16, 8, 128, dtype=F32)]
        + [vmem(16, 128, dtype=F32), vmem(8, 128, dtype=F32)]
        + [dma(4, NC), dma(4, NC), dma(4, NC), dma(5, NC), dma(5, NC), dma(NC), dma(NC), dma(NC, 2), dma(NC, 2), dma(3, NC + 1)]
        + [dma(4), dma(4), dma(4), dma(4), dma(), dma(), dma(), dma(), dma(4), dma(4)]
    )
    results = pl.pallas_call(
        kernel,
        name="monarch_back",
        out_shape=[
            jax.ShapeDtypeStruct((TOKENS, CH), BF16),
            jax.ShapeDtypeStruct((TOKENS, CH), BF16),
            jax.ShapeDtypeStruct((TOKENS, CH), BF16),
            jax.ShapeDtypeStruct((3, 3, CH), F32),
            jax.ShapeDtypeStruct((COLS, COLS), F32),
            jax.ShapeDtypeStruct((256, 256), F32),
            jax.ShapeDtypeStruct((ROWS, COLS), F32),
        ],
        in_specs=[anywhere] * 4 + [inside] * 4,
        out_specs=[anywhere] * 3 + [inside] * 4,
        scratch_shapes=scratch,
        compiler_params=pltpu.CompilerParams(
            collective_id=0, has_side_effects=True, vmem_limit_bytes=VMEM_LIMIT
        ),
    )(flat[0], flat[1], flat[2], flat[3], conv_taps, left_block, right_block, twiddle)
    results = pl.pallas_call(
        write_out,
        name="write_out",
        out_shape=[jax.ShapeDtypeStruct(r.shape, r.dtype) for r in results],
        in_specs=[pl.BlockSpec(memory_space=pltpu.HBM)] * 7,
        out_specs=[pl.BlockSpec(memory_space=pltpu.HBM)] * 7,
        scratch_shapes=[pltpu.VMEM(r.shape, r.dtype) for r in results] + [dma(7, PIECES)] * 2,
        compiler_params=pltpu.CompilerParams(vmem_limit_bytes=VMEM_LIMIT),
    )(*results)
    return tuple(r.reshape(1, TOKENS, CH) for r in results[:3]) + tuple(results[3:])


def solution(mesh):
    rows = P("dp", "seq", None)
    return jax.shard_map(
        shards,
        mesh=mesh,
        in_specs=(rows, rows, rows, rows, P(), P(), P(), P("seq", None)),
        out_specs=(rows, rows, rows, P(), P(), P(), P("seq", None)),
        check_vma=False,
    )
```
